32 devices in a mesh: groups: 2 (over y), gx: 4 (over z), gy: 2 (over x), layer: 2 (over core).
Axes of the slice: x: 2, y: 2, z: 4, core: 2. Of those that a mesh axis runs over, the one named last changes fastest.
Arguments:
- density: bfloat16 [8, 6, 5, 184, 184], P(('groups', 'gx'), 'gy', None, 'layer'), parts along dimension 0
- pattern: int32 [8, 6, 5], P(('groups', 'gx'), 'gy'), parts along dimension 0, may hold values from 0 to 1, as said below
Outputs:
- purified: bfloat16 [8, 6, 5, 184, 184], P(('groups', 'gx'), 'gy', None, 'layer'), parts along dimension 0
The draws below stay inside these ranges and needn't reach their ends.
There are 2 independent parts, one for each index of `groups`. The reference program is written for one: setup_inputs(seed, part) draws one part's arguments, and reference() takes and returns one part's arrays. A program takes and returns all parts, laid end to end along the dimension named above; each array names one. Nothing has to cross between parts.
Inputs may be any that keep to these rules, and one draw needn't show every extreme that they name: `pattern`: slot 0 is always 1; slot 1 of cluster (x, y) equals slot 2 of cluster (x + 1, y), and slot 3 equals slot 4 of cluster (x, y + 1).
All inputs are finite; a program needn't handle non-finite values.
Results may differ from the reference program's by a relative error of at most 0.012.
The reference program's roundings to bfloat16 on the way count: a program that leaves them out, or rounds other values in their place, can miss the bound.
Values may be sent and summed in bfloat16 or wider, within the bound.
A program may use at most 64 MiB of HBM per device.

```python
import jax
import jax.numpy as jnp
from jax import lax

B = 184
STEPS = 2
NX = 4
NY = 6


def draw_density(key, part):
    key = jax.random.fold_in(key, 11)
    noise_key = jax.random.fold_in(key, 0)
    occ_key = jax.random.fold_in(key, 2)
    slot_scale = jnp.array([0.015, 0.045, 0.045, 0.045, 0.045], jnp.float32)[None, None, :, None, None]
    noise = jax.random.normal(noise_key, (NX, NY, 5, B, B), jnp.float32) * slot_scale
    occupied = jax.random.randint(occ_key, (NX, NY, B), 0, 2).astype(jnp.float32)
    diagonal = occupied[:, :, :, None] * jnp.eye(B, dtype=jnp.float32)[None, None]
    full = noise.at[:, :, 0].add(diagonal)
    return full.astype(jnp.bfloat16)


def draw_pattern(key, part):
    key = jax.random.fold_in(key, 23)
    key_x, key_y = jax.random.split(key)
    link_x = jax.random.randint(key_x, (NX, NY), 0, 2).astype(jnp.int32)
    link_y = jax.random.randint(key_y, (NX, NY), 0, 2).astype(jnp.int32)
    center = jnp.ones((NX, NY), jnp.int32)
    return jnp.stack([center, link_x, jnp.roll(link_x, 1, axis=0), link_y, jnp.roll(link_y, 1, axis=1)], -1)


def setup_inputs(seed: int = 0, part: int = 0) -> dict:
    streams_of = jax.random.split(jax.random.key(seed), 3)
    own_keys = jax.random.split(jax.random.fold_in(streams_of[2], part), 3)
    return {
        "density": draw_density(jax.random.fold_in(jax.random.fold_in(streams_of[2], part), 71), part),
        "pattern": draw_pattern(jax.random.fold_in(jax.random.fold_in(streams_of[2], part), 71), part),
    }


OFFSETS = ((0, 0), (1, 0), (-1, 0), (0, 1), (0, -1))
PAIRS = (((0, 0), (1, 2), (2, 1), (3, 4), (4, 3)), ((0, 1), (1, 0)), ((0, 2), (2, 0)), ((0, 3), (3, 0)), ((0, 4), (4, 0)))


def truncated(left, right, keep):
    slots = []
    for pairs in PAIRS:
        total = jnp.zeros(left[:, :, 0].shape, jnp.float32)
        for first, second in pairs:
            shift_x, shift_y = OFFSETS[first]
            partner = jnp.roll(right[:, :, second], (-shift_x, -shift_y), axis=(0, 1))
            total = total + jnp.einsum('xyij,xyjk->xyik', left[:, :, first].astype(jnp.float32), partner.astype(jnp.float32))
        slots.append(total)
    return lax.optimization_barrier((jnp.stack(slots, 2) * keep).astype(jnp.bfloat16))


def reference(density, pattern):
    keep = pattern[:, :, :, None, None].astype(jnp.float32)
    current = density * pattern[:, :, :, None, None].astype(jnp.bfloat16)
    for step in range(STEPS):
        square = truncated(current, current, keep)
        cube = truncated(square, current, keep)
        current = (3.0 * square.astype(jnp.float32) - 2.0 * cube.astype(jnp.float32)).astype(jnp.bfloat16)
    return current
```

```python
import functools

import jax
import jax.numpy as jnp
from jax import lax
from jax.experimental import pallas as pl
from jax.experimental.pallas import tpu as pltpu
from jax.sharding import PartitionSpec as P

STEPS = 2
SLOTS = 5
OPPOSITE = (0, 2, 1, 4, 3)
MESH = pl.DeviceIdType.MESH


def edges_of(count):
    edges = [(a, j, j) for j in range(count) for a in (1, 2)]
    return edges + [(3, count - 1, 0), (4, 0, count - 1)]


def dot(left, right):
    return jnp.dot(left, right, preferred_element_type=jnp.float32)


def kernel(
    keep, density, out, full, pack, halo, acc, square,
    send_l, recv_l, send_h, recv_h, send_r, recv_r,
):
    count, _, rows, columns = density.shape
    high, wide = full.shape[-2:]
    main = wide // 128 * 128
    edges = edges_of(count)
    me = lax.axis_index("layer")
    x, y = lax.axis_index("gx"), lax.axis_index("gy")
    size_x, size_y = lax.axis_size("gx"), lax.axis_size("gy")
    partner = {"layer": 1 - me}
    towards = {
        1: {"gx": lax.rem(x + 1, size_x)},
        2: {"gx": lax.rem(x + size_x - 1, size_x)},
        3: {"gy": lax.rem(y + 1, size_y)},
        4: {"gy": lax.rem(y + size_y - 1, size_y)},
    }

    def local_copy(step, j):
        return pltpu.make_async_remote_copy(
            src_ref=full.at[step, j, :, me], dst_ref=full.at[step, j, :, me],
            send_sem=send_l.at[step, j], recv_sem=recv_l.at[step, j],
            device_id=partner, device_id_type=MESH,
        )

    def halo_copy(step, e):
        return pltpu.make_async_remote_copy(
            src_ref=pack.at[step, e], dst_ref=halo.at[step, e, me],
            send_sem=send_h.at[step, e], recv_sem=recv_h.at[step, e],
            device_id=towards[OPPOSITE[edges[e][0]]], device_id_type=MESH,
        )

    def relay_copy(step, e):
        return pltpu.make_async_remote_copy(
            src_ref=halo.at[step, e, me], dst_ref=halo.at[step, e, me],
            send_sem=send_r.at[step, e], recv_sem=recv_r.at[step, e],
            device_id=partner, device_id_type=MESH,
        )

    def mask(j, s):
        return keep[j * SLOTS + s].astype(jnp.float32)

    def send(step, j, blocks):
        for e, (a, _, source) in enumerate(edges):
            if source == j:
                own, other = blocks[0], blocks[OPPOSITE[a]]
                pack[step, e] = jnp.concatenate(
                    [own[:, :main], other[:, :main], own[:, main:], other[:, main:]], axis=-1
                ).astype(jnp.bfloat16)
                halo_copy(step, e).start()
        for s in range(SLOTS):
            full[step, j, s, me] = blocks[s].astype(jnp.bfloat16)
        local_copy(step, j).start()

    def whole(step, j, s):
        return full[step, j, s].reshape(2 * high, wide)

    def local_terms(step, j, block):
        own = block(0)
        sums = [dot(own, whole(step, j, s)) for s in range(SLOTS)]
        for a, other in ((3, j + 1), (4, j - 1)):
            if 0 <= other < count:
                left = block(a)
                sums[0] = sums[0] + dot(left, whole(step, other, OPPOSITE[a]))
                sums[a] = sums[a] + dot(left, whole(step, other, 0))
        return sums

    def halo_terms(step, j, block, sums):
        for e, (a, user, _) in enumerate(edges):
            if user == j:
                both = dot(block(a), halo[step, e].reshape(2 * high, 2 * wide))
                rest = 2 * main + wide - main
                sums[a] = sums[a] + jnp.concatenate([both[:, :main], both[:, 2 * main : rest]], axis=-1)
                sums[0] = sums[0] + jnp.concatenate([both[:, main : 2 * main], both[:, rest:]], axis=-1)
        return sums

    barrier = pltpu.get_barrier_semaphore()
    for device in (partner, *towards.values()):
        pl.semaphore_signal(barrier, inc=1, device_id=device, device_id_type=MESH)
    pl.semaphore_wait(barrier, 5)

    row = lax.broadcasted_iota(jnp.int32, (columns, wide), 0)
    column = lax.broadcasted_iota(jnp.int32, (columns, wide), 1)
    spread = jnp.where(row + jnp.where(row >= rows, high - rows, 0) == column, 1.0, 0.0).astype(jnp.bfloat16)
    row = lax.broadcasted_iota(jnp.int32, (wide, columns), 0)
    column = lax.broadcasted_iota(jnp.int32, (wide, columns), 1)
    gather = jnp.where(column + jnp.where(column >= rows, high - rows, 0) == row, 1.0, 0.0).astype(jnp.bfloat16)

    for j in range(count):
        blocks = []
        for s in range(SLOTS):
            block = (density[j, s].astype(jnp.float32) * mask(j, s)).astype(jnp.bfloat16)
            block = dot(block, spread)
            blocks.append(jnp.concatenate([block, jnp.zeros((high - rows, wide), jnp.float32)], axis=0))
        send(0, j, blocks)

    for step in range(STEPS):
        for j in range(count):
            local_copy(step, j).wait_recv()
        for j in range(count):
            sums = local_terms(step, j, lambda a: full[step, j, a, me])
            for s in range(SLOTS):
                acc[j, s] = sums[s]
        for j in range(count):
            mine = [e for e in range(len(edges)) if edges[e][1] == j]
            for e in mine:
                halo_copy(step, e).wait_recv()
                relay_copy(step, e).start()
            for e in mine:
                relay_copy(step, e).wait_recv()
            sums = [acc[j, s] for s in range(SLOTS)]
            sums = halo_terms(step, j, lambda a: full[step, j, a, me], sums)
            for s in range(SLOTS):
                square[j, s] = (sums[s] * mask(j, s)).astype(jnp.bfloat16)
            sums = local_terms(step, j, lambda a: square[j, a])
            sums = halo_terms(step, j, lambda a: square[j, a], sums)
            blocks = []
            for s in range(SLOTS):
                cube = (sums[s] * mask(j, s)).astype(jnp.bfloat16).astype(jnp.float32)
                blocks.append(3.0 * square[j, s].astype(jnp.float32) - 2.0 * cube)
            if step < STEPS - 1:
                send(step + 1, j, blocks)
            else:
                for s in range(SLOTS):
                    block = dot(blocks[s].astype(jnp.bfloat16), gather)
                    out[j, s] = block[:rows].astype(jnp.bfloat16)

    for step in range(STEPS):
        for j in range(count):
            local_copy(step, j).wait_send()
        for e in range(len(edges)):
            halo_copy(step, e).wait_send()
            relay_copy(step, e).wait_send()


def on_device(density, pattern):
    _, count, slots, rows, columns = density.shape
    high = -(-rows // 16) * 16
    wide = 2 * high
    number = len(edges_of(count))
    dma = pltpu.SemaphoreType.DMA
    out = pl.pallas_call(
        kernel,
        out_shape=jax.ShapeDtypeStruct((count, slots, rows, columns), jnp.bfloat16),
        in_specs=[pl.BlockSpec(memory_space=pltpu.SMEM), pl.BlockSpec(memory_space=pltpu.VMEM)],
        out_specs=pl.BlockSpec(memory_space=pltpu.VMEM),
        scratch_shapes=[
            pltpu.VMEM((STEPS, count, slots, 2, high, wide), jnp.bfloat16),
            pltpu.VMEM((STEPS, number, high, 2 * wide), jnp.bfloat16),
            pltpu.VMEM((STEPS, number, 2, high, 2 * wide), jnp.bfloat16),
            pltpu.VMEM((count, slots, high, wide), jnp.float32),
            pltpu.VMEM((count, slots, high, wide), jnp.bfloat16),
            dma((STEPS, count)), dma((STEPS, count)),
            dma((STEPS, number)), dma((STEPS, number)),
            dma((STEPS, number)), dma((STEPS, number)),
        ],
        compiler_params=pltpu.CompilerParams(
            collective_id=0, has_side_effects=True, vmem_limit_bytes=40 * 1024 * 1024
        ),
    )(pattern.reshape(-1), density[0])
    return out[None]


def solution(mesh):
    return jax.shard_map(
        on_device,
        mesh=mesh,
        in_specs=(P(("groups", "gx"), "gy", None, "layer", None), P(("groups", "gx"), "gy", None)),
        out_specs=P(("groups", "gx"), "gy", None, "layer", None),
        check_vma=False,
    )
```

```python
import functools

import jax
import jax.numpy as jnp
from jax import lax
from jax.experimental import pallas as pl
from jax.experimental.pallas import tpu as pltpu
from jax.sharding import PartitionSpec as P

STEPS = 2
SLOTS = 5
OPPOSITE = (0, 2, 1, 4, 3)
MESH = pl.DeviceIdType.MESH


def edges_of(count):
    edges = [(a, j, j) for j in range(count) for a in (1, 2)]
    return edges + [(3, count - 1, 0), (4, 0, count - 1)]


def dot(left, right, first=1, second=0):
    return lax.dot_general(
        left, right, (((first,), (second,)), ((), ())), preferred_element_type=jnp.float32
    )


def kernel(
    keep, density, out, full, pack, halo, acc, square,
    send_l, recv_l, send_h, recv_h, send_r, recv_r,
):
    count, _, columns, rows = density.shape
    high, wide = full.shape[-2:]
    main = wide // 128 * 128
    edges = edges_of(count)
    me = lax.axis_index("layer")
    x, y = lax.axis_index("gx"), lax.axis_index("gy")
    size_x, size_y = lax.axis_size("gx"), lax.axis_size("gy")
    partner = {"layer": 1 - me}
    towards = {
        1: {"gx": lax.rem(x + 1, size_x)},
        2: {"gx": lax.rem(x + size_x - 1, size_x)},
        3: {"gy": lax.rem(y + 1, size_y)},
        4: {"gy": lax.rem(y + size_y - 1, size_y)},
    }

    def local_copy(step, j):
        return pltpu.make_async_remote_copy(
            src_ref=full.at[step, j, :, me], dst_ref=full.at[step, j, :, me],
            send_sem=send_l.at[step, j], recv_sem=recv_l.at[step, j],
            device_id=partner, device_id_type=MESH,
        )

    def halo_copy(step, e):
        return pltpu.make_async_remote_copy(
            src_ref=pack.at[step, e], dst_ref=halo.at[step, e, me],
            send_sem=send_h.at[step, e], recv_sem=recv_h.at[step, e],
            device_id=towards[OPPOSITE[edges[e][0]]], device_id_type=MESH,
        )

    def relay_copy(step, e):
        return pltpu.make_async_remote_copy(
            src_ref=halo.at[step, e, me], dst_ref=halo.at[step, e, me],
            send_sem=send_r.at[step, e], recv_sem=recv_r.at[step, e],
            device_id=partner, device_id_type=MESH,
        )

    def mask(j, s):
        return keep[j, 0, s].astype(jnp.float32)

    def send(step, j, blocks):
        for e, (a, _, source) in enumerate(edges):
            if source == j:
                own, other = blocks[0], blocks[OPPOSITE[a]]
                pack[step, e] = jnp.concatenate(
                    [own[:, :main], other[:, :main], own[:, main:], other[:, main:]], axis=-1
                ).astype(jnp.bfloat16)
                halo_copy(step, e).start()
        for s in range(SLOTS):
            full[step, j, s, me] = blocks[s].astype(jnp.bfloat16)
        local_copy(step, j).start()

    def whole(step, j, s):
        return full[step, j, s].reshape(2 * high, wide)

    def local_terms(step, j, block):
        own = block(0)
        sums = [dot(own, whole(step, j, s)) for s in range(SLOTS)]
        for a, other in ((3, j + 1), (4, j - 1)):
            if 0 <= other < count:
                left = block(a)
                sums[0] = sums[0] + dot(left, whole(step, other, OPPOSITE[a]))
                sums[a] = sums[a] + dot(left, whole(step, other, 0))
        return sums

    def halo_terms(step, j, block, sums):
        for e, (a, user, _) in enumerate(edges):
            if user == j:
                both = dot(block(a), halo[step, e].reshape(2 * high, 2 * wide))
                rest = 2 * main + wide - main
                sums[a] = sums[a] + jnp.concatenate([both[:, :main], both[:, 2 * main : rest]], axis=-1)
                sums[0] = sums[0] + jnp.concatenate([both[:, main : 2 * main], both[:, rest:]], axis=-1)
        return sums

    barrier = pltpu.get_barrier_semaphore()
    for device in (partner, *towards.values()):
        pl.semaphore_signal(barrier, inc=1, device_id=device, device_id_type=MESH)
    pl.semaphore_wait(barrier, 5)

    row = lax.broadcasted_iota(jnp.int32, (columns, wide), 0)
    column = lax.broadcasted_iota(jnp.int32, (columns, wide), 1)
    spread = jnp.where(row + jnp.where(row >= rows, high - rows, 0) == column, 1.0, 0.0).astype(jnp.bfloat16)

    for j in range(count):
        blocks = []
        for s in range(SLOTS):
            block = (density[j, s].astype(jnp.float32) * mask(j, s)).astype(jnp.bfloat16)
            block = dot(block, spread, 0, 0)
            blocks.append(jnp.concatenate([block, jnp.zeros((high - rows, wide), jnp.float32)], axis=0))
        send(0, j, blocks)

    for step in range(STEPS):
        for j in range(count):
            local_copy(step, j).wait_recv()
        for j in range(count):
            sums = local_terms(step, j, lambda a: full[step, j, a, me])
            for s in range(SLOTS):
                acc[j, s] = sums[s]
        for j in range(count):
            mine = [e for e in range(len(edges)) if edges[e][1] == j]
            for e in mine:
                halo_copy(step, e).wait_recv()
                relay_copy(step, e).start()
            for e in mine:
                relay_copy(step, e).wait_recv()
            sums = [acc[j, s] for s in range(SLOTS)]
            sums = halo_terms(step, j, lambda a: full[step, j, a, me], sums)
            for s in range(SLOTS):
                square[j, s] = (sums[s] * mask(j, s)).astype(jnp.bfloat16)
            sums = local_terms(step, j, lambda a: square[j, a])
            sums = halo_terms(step, j, lambda a: square[j, a], sums)
            blocks = []
            for s in range(SLOTS):
                cube = (sums[s] * mask(j, s)).astype(jnp.bfloat16).astype(jnp.float32)
                blocks.append(3.0 * square[j, s].astype(jnp.float32) - 2.0 * cube)
            if step < STEPS - 1:
                send(step + 1, j, blocks)
            else:
                for s in range(SLOTS):
                    block = dot(spread, blocks[s].astype(jnp.bfloat16), 1, 1)
                    out[j, s] = block[:, :rows].astype(jnp.bfloat16)

    for step in range(STEPS):
        for j in range(count):
            local_copy(step, j).wait_send()
        for e in range(len(edges)):
            halo_copy(step, e).wait_send()
            relay_copy(step, e).wait_send()


def on_device(density, pattern):
    _, count, slots, rows, columns = density.shape
    high = -(-rows // 16) * 16
    wide = 2 * high
    number = len(edges_of(count))
    dma = pltpu.SemaphoreType.DMA
    out = pl.pallas_call(
        kernel,
        out_shape=jax.ShapeDtypeStruct((count, slots, columns, rows), jnp.bfloat16),
        in_specs=[pl.BlockSpec(memory_space=pltpu.SMEM), pl.BlockSpec(memory_space=pltpu.VMEM)],
        out_specs=pl.BlockSpec(memory_space=pltpu.VMEM),
        scratch_shapes=[
            pltpu.VMEM((STEPS, count, slots, 2, high, wide), jnp.bfloat16),
            pltpu.VMEM((STEPS, number, high, 2 * wide), jnp.bfloat16),
            pltpu.VMEM((STEPS, number, 2, high, 2 * wide), jnp.bfloat16),
            pltpu.VMEM((count, slots, high, wide), jnp.float32),
            pltpu.VMEM((count, slots, high, wide), jnp.bfloat16),
            dma((STEPS, count)), dma((STEPS, count)),
            dma((STEPS, number)), dma((STEPS, number)),
            dma((STEPS, number)), dma((STEPS, number)),
        ],
        compiler_params=pltpu.CompilerParams(
            collective_id=0, has_side_effects=True, vmem_limit_bytes=40 * 1024 * 1024
        ),
    )(jnp.swapaxes(pattern, 0, 1), jnp.swapaxes(density[0], 2, 3))
    return jnp.swapaxes(out, 2, 3)[None]


def solution(mesh):
    return jax.shard_map(
        on_device,
        mesh=mesh,
        in_specs=(P(("groups", "gx"), "gy", None, "layer", None), P(("groups", "gx"), "gy", None)),
        out_specs=P(("groups", "gx"), "gy", None, "layer", None),
        check_vma=False,
    )
```

```python
import functools

import jax
import jax.numpy as jnp
from jax import lax
from jax.experimental import pallas as pl
from jax.experimental.pallas import tpu as pltpu
from jax.sharding import PartitionSpec as P

STEPS = 2
SLOTS = 5
OPPOSITE = (0, 2, 1, 4, 3)
MESH = pl.DeviceIdType.MESH


def edges_of(count):
    edges = [(a, j, j) for j in range(count) for a in (1, 2)]
    return edges + [(3, count - 1, 0), (4, 0, count - 1)]


def dot(left, right, first=1, second=0):
    return lax.dot_general(
        left, right, (((first,), (second,)), ((), ())), preferred_element_type=jnp.float32
    )


def kernel(
    pattern, density, out, full, pack, halo, acc, square, keep, staged,
    send_l, recv_l, send_h, recv_h, send_r, recv_r, load, load_keep,
):
    count, _, columns, rows = density.shape
    high, wide = full.shape[-2:]
    main = wide // 128 * 128
    edges = edges_of(count)
    me = lax.axis_index("layer")
    x, y = lax.axis_index("gx"), lax.axis_index("gy")
    size_x, size_y = lax.axis_size("gx"), lax.axis_size("gy")
    partner = {"layer": 1 - me}
    towards = {
        1: {"gx": lax.rem(x + 1, size_x)},
        2: {"gx": lax.rem(x + size_x - 1, size_x)},
        3: {"gy": lax.rem(y + 1, size_y)},
        4: {"gy": lax.rem(y + size_y - 1, size_y)},
    }

    def local_copy(step, j):
        return pltpu.make_async_remote_copy(
            src_ref=full.at[step, j, :, me], dst_ref=full.at[step, j, :, me],
            send_sem=send_l.at[step, j], recv_sem=recv_l.at[step, j],
            device_id=partner, device_id_type=MESH,
        )

    def halo_copy(step, e):
        return pltpu.make_async_remote_copy(
            src_ref=pack.at[step, e], dst_ref=halo.at[step, e, me],
            send_sem=send_h.at[step, e], recv_sem=recv_h.at[step, e],
            device_id=towards[OPPOSITE[edges[e][0]]], device_id_type=MESH,
        )

    def relay_copy(step, e):
        return pltpu.make_async_remote_copy(
            src_ref=halo.at[step, e, me], dst_ref=halo.at[step, e, me],
            send_sem=send_r.at[step, e], recv_sem=recv_r.at[step, e],
            device_id=partner, device_id_type=MESH,
        )

    def mask(j, s):
        return keep[j, 0, s].astype(jnp.float32)

    def send_halo(step, j, blocks, slots):
        for e, (a, _, source) in enumerate(edges):
            if source == j and a in slots:
                own, other = blocks[0], blocks[OPPOSITE[a]]
                pack[step, e] = jnp.concatenate(
                    [own[:, :main], other[:, :main], own[:, main:], other[:, main:]], axis=-1
                ).astype(jnp.bfloat16)
                halo_copy(step, e).start()

    def store(step, j, blocks, slots):
        for s in slots:
            full[step, j, s, me] = blocks[s].astype(jnp.bfloat16)

    def whole(step, j, s):
        return full[step, j, s].reshape(2 * high, wide)

    def local_terms(step, j, block):
        own = block(0)
        sums = [dot(own, whole(step, j, s)) for s in range(SLOTS)]
        for a, other in ((3, j + 1), (4, j - 1)):
            if 0 <= other < count:
                left = block(a)
                sums[0] = sums[0] + dot(left, whole(step, other, OPPOSITE[a]))
                sums[a] = sums[a] + dot(left, whole(step, other, 0))
        return sums

    def halo_terms(step, j, block, sums):
        for e, (a, user, _) in enumerate(edges):
            if user == j:
                both = dot(block(a), halo[step, e].reshape(2 * high, 2 * wide))
                rest = 2 * main + wide - main
                sums[a] = sums[a] + jnp.concatenate([both[:, :main], both[:, 2 * main : rest]], axis=-1)
                sums[0] = sums[0] + jnp.concatenate([both[:, main : 2 * main], both[:, rest:]], axis=-1)
        return sums

    barrier = pltpu.get_barrier_semaphore()
    for device in (partner, *towards.values()):
        pl.semaphore_signal(barrier, inc=1, device_id=device, device_id_type=MESH)
    loads = [pltpu.make_async_copy(density.at[j], staged.at[j], load.at[j]) for j in range(count)]
    load_pattern = pltpu.make_async_copy(pattern, keep, load_keep)
    load_pattern.start()
    for copy in loads:
        copy.start()

    row = lax.broadcasted_iota(jnp.int32, (columns, wide), 0)
    column = lax.broadcasted_iota(jnp.int32, (columns, wide), 1)
    spread = jnp.where(row + jnp.where(row >= rows, high - rows, 0) == column, 1.0, 0.0).astype(jnp.bfloat16)

    load_pattern.wait()

    def begin(j, s):
        block = (staged[j, s].astype(jnp.float32) * mask(j, s)).astype(jnp.bfloat16)
        block = dot(block, spread, 0, 0)
        return jnp.concatenate([block, jnp.zeros((high - rows, wide), jnp.float32)], axis=0)

    for j in range(count):
        loads[j].wait()
        blocks = [begin(j, s) for s in range(3)]
        if j == 0:
            pl.semaphore_wait(barrier, 5)
        send_halo(0, j, blocks, (1, 2))
        store(0, j, blocks, range(3))
    for j in range(count):
        blocks = [begin(j, s) if s % 3 == 0 or s == 4 else None for s in range(SLOTS)]
        send_halo(0, j, blocks, (3, 4))
        store(0, j, blocks, (3, 4))
        local_copy(0, j).start()

    for step in range(STEPS):
        for j in range(count):
            local_copy(step, j).wait_recv()
        for j in range(count):
            sums = local_terms(step, j, lambda a: full[step, j, a, me])
            for s in range(SLOTS):
                acc[j, s] = sums[s]
        for j in range(count):
            mine = [e for e in range(len(edges)) if edges[e][1] == j]
            for e in mine:
                halo_copy(step, e).wait_recv()
                relay_copy(step, e).start()
            for e in mine:
                relay_copy(step, e).wait_recv()
            sums = [acc[j, s] for s in range(SLOTS)]
            sums = halo_terms(step, j, lambda a: full[step, j, a, me], sums)
            for s in range(SLOTS):
                square[j, s] = (sums[s] * mask(j, s)).astype(jnp.bfloat16)
            sums = local_terms(step, j, lambda a: square[j, a])
            sums = halo_terms(step, j, lambda a: square[j, a], sums)
            blocks = []
            for s in range(SLOTS):
                cube = (sums[s] * mask(j, s)).astype(jnp.bfloat16).astype(jnp.float32)
                blocks.append(3.0 * square[j, s].astype(jnp.float32) - 2.0 * cube)
            if step < STEPS - 1:
                send_halo(step + 1, j, blocks, (1, 2, 3, 4))
                store(step + 1, j, blocks, range(SLOTS))
                local_copy(step + 1, j).start()
            else:
                for s in range(SLOTS):
                    block = dot(spread, blocks[s].astype(jnp.bfloat16), 1, 1)
                    out[j, s] = block[:, :rows].astype(jnp.bfloat16)

    for step in range(STEPS):
        for j in range(count):
            local_copy(step, j).wait_send()
        for e in range(len(edges)):
            halo_copy(step, e).wait_send()
            relay_copy(step, e).wait_send()


def on_device(density, pattern):
    _, count, slots, rows, columns = density.shape
    high = -(-rows // 16) * 16
    wide = 2 * high
    number = len(edges_of(count))
    dma = pltpu.SemaphoreType.DMA
    out = pl.pallas_call(
        kernel,
        out_shape=pltpu.VMEM((count, slots, columns, rows), jnp.bfloat16),
        in_specs=[pl.BlockSpec(memory_space=pltpu.HBM)] * 2,
        out_specs=pl.BlockSpec(memory_space=pltpu.VMEM),
        scratch_shapes=[
            pltpu.VMEM((STEPS, count, slots, 2, high, wide), jnp.bfloat16),
            pltpu.VMEM((STEPS, number, high, 2 * wide), jnp.bfloat16),
            pltpu.VMEM((STEPS, number, 2, high, 2 * wide), jnp.bfloat16),
            pltpu.VMEM((count, slots, high, wide), jnp.float32),
            pltpu.VMEM((count, slots, high, wide), jnp.bfloat16),
            pltpu.SMEM((count, 1, slots), jnp.int32),
            pltpu.VMEM((count, slots, columns, rows), jnp.bfloat16),
            dma((STEPS, count)), dma((STEPS, count)),
            dma((STEPS, number)), dma((STEPS, number)),
            dma((STEPS, number)), dma((STEPS, number)),
            dma((count,)), dma,
        ],
        compiler_params=pltpu.CompilerParams(
            collective_id=0, has_side_effects=True, vmem_limit_bytes=60 * 1024 * 1024
        ),
    )(jnp.swapaxes(pattern, 0, 1), jnp.swapaxes(density[0], 2, 3))
    return jnp.swapaxes(out, 2, 3)[None]


def solution(mesh):
    return jax.shard_map(
        on_device,
        mesh=mesh,
        in_specs=(P(("groups", "gx"), "gy", None, "layer", None), P(("groups", "gx"), "gy", None)),
        out_specs=P(("groups", "gx"), "gy", None, "layer", None),
        check_vma=False,
    )
```

```python
import functools

import jax
import jax.numpy as jnp
from jax import lax
from jax.experimental import pallas as pl
from jax.experimental.pallas import tpu as pltpu
from jax.sharding import PartitionSpec as P

STEPS = 2
SLOTS = 5
OPPOSITE = (0, 2, 1, 4, 3)
MESH = pl.DeviceIdType.MESH


def edges_of(count):
    edges = [(a, j, j) for j in range(count) for a in (1, 2)]
    return edges + [(3, count - 1, 0), (4, 0, count - 1)]


def dot(left, right, first=1, second=0):
    return lax.dot_general(
        left, right, (((first,), (second,)), ((), ())), preferred_element_type=jnp.float32
    )


def kernel(
    pattern, density, out, full, pack, halo, acc, square, keep, staged,
    send_l, recv_l, send_h, recv_h, send_r, recv_r, load, load_keep,
):
    count, _, columns, rows = density.shape
    high, wide = full.shape[-2:]
    main = wide // 128 * 128
    edges = edges_of(count)
    me = lax.axis_index("layer")
    x, y = lax.axis_index("gx"), lax.axis_index("gy")
    size_x, size_y = lax.axis_size("gx"), lax.axis_size("gy")
    partner = {"layer": 1 - me}
    towards = {
        1: {"gx": lax.rem(x + 1, size_x)},
        2: {"gx": lax.rem(x + size_x - 1, size_x)},
        3: {"gy": lax.rem(y + 1, size_y)},
        4: {"gy": lax.rem(y + size_y - 1, size_y)},
    }

    def local_copy(step, j):
        return pltpu.make_async_remote_copy(
            src_ref=full.at[step, j, :, me], dst_ref=full.at[step, j, :, me],
            send_sem=send_l.at[step, j], recv_sem=recv_l.at[step, j],
            device_id=partner, device_id_type=MESH,
        )

    def halo_copy(step, e):
        return pltpu.make_async_remote_copy(
            src_ref=pack.at[step, e], dst_ref=halo.at[step, e, me],
            send_sem=send_h.at[step, e], recv_sem=recv_h.at[step, e],
            device_id=towards[OPPOSITE[edges[e][0]]], device_id_type=MESH,
        )

    def relay_copy(step, e):
        return pltpu.make_async_remote_copy(
            src_ref=halo.at[step, e, me], dst_ref=halo.at[step, e, me],
            send_sem=send_r.at[step, e], recv_sem=recv_r.at[step, e],
            device_id=partner, device_id_type=MESH,
        )

    def mask(j, s):
        return keep[j, 0, s].astype(jnp.float32)

    def pack_halo(step, j, blocks, slots):
        for e, (a, _, source) in enumerate(edges):
            if source == j and a in slots:
                own, other = blocks[0], blocks[OPPOSITE[a]]
                pack[step, e] = jnp.concatenate(
                    [own[:, :main], other[:, :main], own[:, main:], other[:, main:]], axis=-1
                ).astype(jnp.bfloat16)

    def send_halo(step, j, slots):
        for a in slots:
            for e, edge in enumerate(edges):
                if edge[0] == a and edge[2] == j:
                    halo_copy(step, e).start()

    def send_x(step, j):
        pl.when(x == size_x - 1)(lambda: send_halo(step, j, (2, 1)))
        pl.when(x != size_x - 1)(lambda: send_halo(step, j, (1, 2)))

    def store(step, j, blocks, slots):
        for s in slots:
            full[step, j, s, me] = blocks[s].astype(jnp.bfloat16)

    def whole(step, j, s):
        return full[step, j, s].reshape(2 * high, wide)

    def local_terms(step, j, block):
        own = block(0)
        sums = [dot(own, whole(step, j, s)) for s in range(SLOTS)]
        for a, other in ((3, j + 1), (4, j - 1)):
            if 0 <= other < count:
                left = block(a)
                sums[0] = sums[0] + dot(left, whole(step, other, OPPOSITE[a]))
                sums[a] = sums[a] + dot(left, whole(step, other, 0))
        return sums

    def halo_terms(step, j, block, sums):
        for e, (a, user, _) in enumerate(edges):
            if user == j:
                both = dot(block(a), halo[step, e].reshape(2 * high, 2 * wide))
                rest = 2 * main + wide - main
                sums[a] = sums[a] + jnp.concatenate([both[:, :main], both[:, 2 * main : rest]], axis=-1)
                sums[0] = sums[0] + jnp.concatenate([both[:, main : 2 * main], both[:, rest:]], axis=-1)
        return sums

    barrier = pltpu.get_barrier_semaphore()
    for device in (partner, *towards.values()):
        pl.semaphore_signal(barrier, inc=1, device_id=device, device_id_type=MESH)
    loads = [pltpu.make_async_copy(density.at[j], staged.at[j], load.at[j]) for j in range(count)]
    load_pattern = pltpu.make_async_copy(pattern, keep, load_keep)
    load_pattern.start()
    for copy in loads:
        copy.start()

    row = lax.broadcasted_iota(jnp.int32, (columns, wide), 0)
    column = lax.broadcasted_iota(jnp.int32, (columns, wide), 1)
    spread = jnp.where(row + jnp.where(row >= rows, high - rows, 0) == column, 1.0, 0.0).astype(jnp.bfloat16)

    load_pattern.wait()

    def begin(j, s):
        block = (staged[j, s].astype(jnp.float32) * mask(j, s)).astype(jnp.bfloat16)
        block = dot(block, spread, 0, 0)
        return jnp.concatenate([block, jnp.zeros((high - rows, wide), jnp.float32)], axis=0)

    for j in range(count):
        loads[j].wait()
        blocks = [begin(j, s) for s in range(3)]
        pack_halo(0, j, blocks, (1, 2))
        if j == 0:
            pl.semaphore_wait(barrier, 5)
        send_x(0, j)
        store(0, j, blocks, range(3))
    for j in range(count):
        blocks = [begin(j, s) if s % 3 == 0 or s == 4 else None for s in range(SLOTS)]
        pack_halo(0, j, blocks, (3, 4))
        send_halo(0, j, (3, 4))
        store(0, j, blocks, (3, 4))
        local_copy(0, j).start()

    for step in range(STEPS):
        for j in range(count):
            local_copy(step, j).wait_recv()
        for j in range(count):
            sums = local_terms(step, j, lambda a: full[step, j, a, me])
            for s in range(SLOTS):
                acc[j, s] = sums[s]
        for j in range(count):
            mine = [e for e in range(len(edges)) if edges[e][1] == j]
            for e in mine:
                halo_copy(step, e).wait_recv()
                relay_copy(step, e).start()
            for e in mine:
                relay_copy(step, e).wait_recv()
            sums = [acc[j, s] for s in range(SLOTS)]
            sums = halo_terms(step, j, lambda a: full[step, j, a, me], sums)
            for s in range(SLOTS):
                square[j, s] = (sums[s] * mask(j, s)).astype(jnp.bfloat16)
            sums = local_terms(step, j, lambda a: square[j, a])
            sums = halo_terms(step, j, lambda a: square[j, a], sums)
            blocks = []
            for s in range(SLOTS):
                cube = (sums[s] * mask(j, s)).astype(jnp.bfloat16).astype(jnp.float32)
                blocks.append(3.0 * square[j, s].astype(jnp.float32) - 2.0 * cube)
            if step < STEPS - 1:
                pack_halo(step + 1, j, blocks, (1, 2, 3, 4))
                send_x(step + 1, j)
                send_halo(step + 1, j, (3, 4))
                store(step + 1, j, blocks, range(SLOTS))
                local_copy(step + 1, j).start()
            else:
                for s in range(SLOTS):
                    block = dot(spread, blocks[s].astype(jnp.bfloat16), 1, 1)
                    out[j, s] = block[:, :rows].astype(jnp.bfloat16)

    for step in range(STEPS):
        for j in range(count):
            local_copy(step, j).wait_send()
        for e in range(len(edges)):
            halo_copy(step, e).wait_send()
            relay_copy(step, e).wait_send()


def on_device(density, pattern):
    _, count, slots, rows, columns = density.shape
    high = -(-rows // 16) * 16
    wide = 2 * high
    number = len(edges_of(count))
    dma = pltpu.SemaphoreType.DMA
    out = pl.pallas_call(
        kernel,
        out_shape=pltpu.VMEM((count, slots, columns, rows), jnp.bfloat16),
        in_specs=[pl.BlockSpec(memory_space=pltpu.HBM)] * 2,
        out_specs=pl.BlockSpec(memory_space=pltpu.VMEM),
        scratch_shapes=[
            pltpu.VMEM((STEPS, count, slots, 2, high, wide), jnp.bfloat16),
            pltpu.VMEM((STEPS, number, high, 2 * wide), jnp.bfloat16),
            pltpu.VMEM((STEPS, number, 2, high, 2 * wide), jnp.bfloat16),
            pltpu.VMEM((count, slots, high, wide), jnp.float32),
            pltpu.VMEM((count, slots, high, wide), jnp.bfloat16),
            pltpu.SMEM((count, 1, slots), jnp.int32),
            pltpu.VMEM((count, slots, columns, rows), jnp.bfloat16),
            dma((STEPS, count)), dma((STEPS, count)),
            dma((STEPS, number)), dma((STEPS, number)),
            dma((STEPS, number)), dma((STEPS, number)),
            dma((count,)), dma,
        ],
        compiler_params=pltpu.CompilerParams(
            collective_id=0, has_side_effects=True, vmem_limit_bytes=60 * 1024 * 1024
        ),
    )(jnp.swapaxes(pattern, 0, 1), jnp.swapaxes(density[0], 2, 3))
    return jnp.swapaxes(out, 2, 3)[None]


def solution(mesh):
    return jax.shard_map(
        on_device,
        mesh=mesh,
        in_specs=(P(("groups", "gx"), "gy", None, "layer", None), P(("groups", "gx"), "gy", None)),
        out_specs=P(("groups", "gx"), "gy", None, "layer", None),
        check_vma=False,
    )
```

```python
import functools

import jax
import jax.numpy as jnp
from jax import lax
from jax.experimental import pallas as pl
from jax.experimental.pallas import tpu as pltpu
from jax.sharding import PartitionSpec as P

STEPS = 2
SLOTS = 5
OPPOSITE = (0, 2, 1, 4, 3)
MESH = pl.DeviceIdType.MESH


def edges_of(count):
    edges = [(a, j, j) for j in range(count) for a in (1, 2)]
    return edges + [(3, count - 1, 0), (4, 0, count - 1)]


def dot(left, right, first=1, second=0):
    return lax.dot_general(
        left, right, (((first,), (second,)), ((), ())), preferred_element_type=jnp.float32
    )


def kernel(
    pattern, density, out, full, pack, halo, acc, square, keep, staged,
    send_l, recv_l, send_h, recv_h, send_r, recv_r, load, load_keep,
):
    count, _, columns, rows = density.shape
    high, wide = full.shape[-2:]
    main = wide // 128 * 128
    edges = edges_of(count)
    order = (0, *range(count - 1, 0, -1))
    me = lax.axis_index("layer")
    x, y = lax.axis_index("gx"), lax.axis_index("gy")
    size_x, size_y = lax.axis_size("gx"), lax.axis_size("gy")
    partner = {"layer": 1 - me}
    towards = {
        1: {"gx": lax.rem(x + 1, size_x)},
        2: {"gx": lax.rem(x + size_x - 1, size_x)},
        3: {"gy": lax.rem(y + 1, size_y)},
        4: {"gy": lax.rem(y + size_y - 1, size_y)},
    }

    def local_copy(step, j):
        return pltpu.make_async_remote_copy(
            src_ref=full.at[step, j, :, me], dst_ref=full.at[step, j, :, me],
            send_sem=send_l.at[step, j], recv_sem=recv_l.at[step, j],
            device_id=partner, device_id_type=MESH,
        )

    def halo_copy(step, e):
        return pltpu.make_async_remote_copy(
            src_ref=pack.at[step, e], dst_ref=halo.at[step, e, me],
            send_sem=send_h.at[step, e], recv_sem=recv_h.at[step, e],
            device_id=towards[OPPOSITE[edges[e][0]]], device_id_type=MESH,
        )

    def relay_copy(step, e):
        return pltpu.make_async_remote_copy(
            src_ref=halo.at[step, e, me], dst_ref=halo.at[step, e, me],
            send_sem=send_r.at[step, e], recv_sem=recv_r.at[step, e],
            device_id=partner, device_id_type=MESH,
        )

    def mask(j, s):
        return keep[j, 0, s].astype(jnp.float32)

    def pack_halo(step, j, blocks, slots):
        for e, (a, _, source) in enumerate(edges):
            if source == j and a in slots:
                own, other = blocks[0], blocks[OPPOSITE[a]]
                pack[step, e] = jnp.concatenate(
                    [own[:, :main], other[:, :main], own[:, main:], other[:, main:]], axis=-1
                ).astype(jnp.bfloat16)

    def send_halo(step, j, slots):
        for a in slots:
            for e, edge in enumerate(edges):
                if edge[0] == a and edge[2] == j:
                    halo_copy(step, e).start()

    def send_x(step, j):
        pl.when(x == size_x - 1)(lambda: send_halo(step, j, (2, 1)))
        pl.when(x != size_x - 1)(lambda: send_halo(step, j, (1, 2)))

    def store(step, j, blocks, slots):
        for s in slots:
            full[step, j, s, me] = blocks[s].astype(jnp.bfloat16)

    def whole(step, j, s):
        return full[step, j, s].reshape(2 * high, wide)

    def local_terms(step, j, block):
        own = block(0)
        sums = [dot(own, whole(step, j, s)) for s in range(SLOTS)]
        for a, other in ((3, j + 1), (4, j - 1)):
            if 0 <= other < count:
                left = block(a)
                sums[0] = sums[0] + dot(left, whole(step, other, OPPOSITE[a]))
                sums[a] = sums[a] + dot(left, whole(step, other, 0))
        return sums

    def halo_terms(step, j, block, sums):
        for e, (a, user, _) in enumerate(edges):
            if user == j:
                both = dot(block(a), halo[step, e].reshape(2 * high, 2 * wide))
                rest = 2 * main + wide - main
                sums[a] = sums[a] + jnp.concatenate([both[:, :main], both[:, 2 * main : rest]], axis=-1)
                sums[0] = sums[0] + jnp.concatenate([both[:, main : 2 * main], both[:, rest:]], axis=-1)
        return sums

    barrier = pltpu.get_barrier_semaphore()
    for device in (partner, *towards.values()):
        pl.semaphore_signal(barrier, inc=1, device_id=device, device_id_type=MESH)
    parts = [(j, p) for p in range(2) for j in order]
    loads = {
        (j, p): pltpu.make_async_copy(
            density.at[j, pl.ds(3 * p, 3 - p)], staged.at[j, pl.ds(3 * p, 3 - p)], load.at[j, p]
        )
        for j, p in parts
    }
    load_pattern = pltpu.make_async_copy(pattern, keep, load_keep)
    load_pattern.start()
    for part in parts:
        loads[part].start()

    row = lax.broadcasted_iota(jnp.int32, (columns, wide), 0)
    column = lax.broadcasted_iota(jnp.int32, (columns, wide), 1)
    spread = jnp.where(row + jnp.where(row >= rows, high - rows, 0) == column, 1.0, 0.0).astype(jnp.bfloat16)

    load_pattern.wait()

    def begin(j, s):
        block = (staged[j, s].astype(jnp.float32) * mask(j, s)).astype(jnp.bfloat16)
        block = dot(block, spread, 0, 0)
        return jnp.concatenate([block, jnp.zeros((high - rows, wide), jnp.float32)], axis=0)

    for j in order:
        loads[j, 0].wait()
        blocks = [begin(j, s) for s in range(3)]
        pack_halo(0, j, blocks, (1, 2))
        if j == 0:
            pl.semaphore_wait(barrier, 5)
        send_x(0, j)
        store(0, j, blocks, range(3))
    for j in order:
        loads[j, 1].wait()
        blocks = [begin(j, s) if s % 3 == 0 or s == 4 else None for s in range(SLOTS)]
        pack_halo(0, j, blocks, (3, 4))
        send_halo(0, j, (3, 4))
        store(0, j, blocks, (3, 4))
        local_copy(0, j).start()

    for step in range(STEPS):
        for j in range(count):
            local_copy(step, j).wait_recv()
        for j in range(count):
            sums = local_terms(step, j, lambda a: full[step, j, a, me])
            for s in range(SLOTS):
                acc[j, s] = sums[s]
        for j in order:
            mine = [e for e in range(len(edges)) if edges[e][1] == j]
            for e in mine:
                halo_copy(step, e).wait_recv()
                relay_copy(step, e).start()
            for e in mine:
                relay_copy(step, e).wait_recv()
            sums = [acc[j, s] for s in range(SLOTS)]
            sums = halo_terms(step, j, lambda a: full[step, j, a, me], sums)
            for s in range(SLOTS):
                square[j, s] = (sums[s] * mask(j, s)).astype(jnp.bfloat16)
            sums = local_terms(step, j, lambda a: square[j, a])
            sums = halo_terms(step, j, lambda a: square[j, a], sums)
            blocks = []
            for s in range(SLOTS):
                cube = (sums[s] * mask(j, s)).astype(jnp.bfloat16).astype(jnp.float32)
                blocks.append(3.0 * square[j, s].astype(jnp.float32) - 2.0 * cube)
            if step < STEPS - 1:
                pack_halo(step + 1, j, blocks, (1, 2, 3, 4))
                send_x(step + 1, j)
                send_halo(step + 1, j, (3, 4))
                store(step + 1, j, blocks, range(SLOTS))
                local_copy(step + 1, j).start()
            else:
                for s in range(SLOTS):
                    block = dot(spread, blocks[s].astype(jnp.bfloat16), 1, 1)
                    out[j, s] = block[:, :rows].astype(jnp.bfloat16)

    for step in range(STEPS):
        for j in range(count):
            local_copy(step, j).wait_send()
        for e in range(len(edges)):
            halo_copy(step, e).wait_send()
            relay_copy(step, e).wait_send()


def on_device(density, pattern):
    _, count, slots, rows, columns = density.shape
    high = -(-rows // 16) * 16
    wide = 2 * high
    number = len(edges_of(count))
    dma = pltpu.SemaphoreType.DMA
    out = pl.pallas_call(
        kernel,
        out_shape=pltpu.VMEM((count, slots, columns, rows), jnp.bfloat16),
        in_specs=[pl.BlockSpec(memory_space=pltpu.HBM)] * 2,
        out_specs=pl.BlockSpec(memory_space=pltpu.VMEM),
        scratch_shapes=[
            pltpu.VMEM((STEPS, count, slots, 2, high, wide), jnp.bfloat16),
            pltpu.VMEM((STEPS, number, high, 2 * wide), jnp.bfloat16),
            pltpu.VMEM((STEPS, number, 2, high, 2 * wide), jnp.bfloat16),
            pltpu.VMEM((count, slots, high, wide), jnp.float32),
            pltpu.VMEM((count, slots, high, wide), jnp.bfloat16),
            pltpu.SMEM((count, 1, slots), jnp.int32),
            pltpu.VMEM((count, slots, columns, rows), jnp.bfloat16),
            dma((STEPS, count)), dma((STEPS, count)),
            dma((STEPS, number)), dma((STEPS, number)),
            dma((STEPS, number)), dma((STEPS, number)),
            dma((count, 2)), dma,
        ],
        compiler_params=pltpu.CompilerParams(
            collective_id=0, has_side_effects=True, vmem_limit_bytes=60 * 1024 * 1024
        ),
    )(jnp.swapaxes(pattern, 0, 1), jnp.swapaxes(density[0], 2, 3))
    return jnp.swapaxes(out, 2, 3)[None]


def solution(mesh):
    return jax.shard_map(
        on_device,
        mesh=mesh,
        in_specs=(P(("groups", "gx"), "gy", None, "layer", None), P(("groups", "gx"), "gy", None)),
        out_specs=P(("groups", "gx"), "gy", None, "layer", None),
        check_vma=False,
    )
```
